128 devices in a mesh: stream: 16 (over x_lo, z, core), span: 8 (over y, x_hi).
Axes of the slice: x: 4 (x_hi: 2, x_lo: 2; x = x_hi * 2 + x_lo), y: 4, z: 4, core: 2. Of those that a mesh axis runs over, the one named last changes fastest.
Arguments:
- main_flow: float32 [3, 192, 256, 1024], P(None, 'stream', 'span'), may hold values from -6 to 6
- precursor: float32 [3, 256, 256, 1024], P(None, 'stream', 'span'), may hold values from -6 to 6
- magnet_field: float32 [3, 192, 256, 1024], P(None, 'stream', 'span'), may hold values from -6 to 6
- inlet_rows: int32 [256], replicated, may hold values from 0 to 255, each once
Outputs:
- main_next: float32 [3, 192, 256, 1024], P(None, 'stream', 'span')
- precursor_next: float32 [3, 256, 256, 1024], P(None, 'stream', 'span')
The draws below stay inside these ranges and needn't reach their ends.
Inputs may be any that keep to these rules, and one draw needn't show every extreme that they name: `inlet_rows`: a permutation of the spanwise rows.
All inputs are finite; a program needn't handle non-finite values.
Results may differ from the reference program's by a relative error of at most 0.0001.
Values sent between devices are 32-bit elements; how exact they have to be, the bound alone decides.
No kernel may reach another device: no remote copies, remote signals or barrier semaphores. Data moves between devices by JAX's collectives and lax.ppermute only.
A program may use at most 128 MiB of HBM per device.

```python
import jax
import jax.numpy as jnp
from jax import lax

CX = 12
PCX = 16
NZ = 1024
NX = 192
PX = 256
NY = 256


def levels(rng, shape, shards, low, largest):
    gain = 1.0
    for position, blocks in shards:
        draws = jax.random.uniform(jax.random.fold_in(jax.random.fold_in(rng, 6), position), (blocks,), jnp.float32, low / len(shards), largest / len(shards))
        gain = gain * jnp.repeat(jnp.exp(draws), shape[position] // blocks).reshape((-1,) + (1,) * (len(shape) - 1 - position))
    return gain


def gaussian(key, shape, width, limit, shards=(), held_as=jnp.bfloat16):
    array = jax.random.normal(key, shape, jnp.float32) * width
    if len(shards) > 0:
        array = levels(key, shape, shards, -0.22, 0.18) * array
    return jnp.clip(array, min=-limit, max=limit).astype(held_as)


def setup_inputs(seed: int = 0) -> dict:
    key_list = jax.random.split(jax.random.key(seed), 5)
    main_flow = gaussian(key_list[0], (3, NX, NY, NZ), 1.0, 6.0, ((1, 16), (2, 8)), jnp.float32)
    precursor = gaussian(key_list[1], (3, PX, NY, NZ), 1.0, 6.0, ((1, 16), (2, 8)), jnp.float32)
    magnet_field = gaussian(key_list[2], (3, NX, NY, NZ), 1.0, 6.0, ((1, 16), (2, 8)), jnp.float32)
    inlet_rows = jax.random.permutation(key_list[3], NY).astype(jnp.int32)
    return {"main_flow": main_flow, "precursor": precursor, "magnet_field": magnet_field, "inlet_rows": inlet_rows}


TIME_STEP = 0.1
VISCOSITY = 0.02
SMAGORINSKY = 0.03
INTERACTION = 0.5

def tendency(center, stream_ext, span_ext):
    padded = jnp.pad(center, ((0, 0), (0, 0), (0, 0), (1, 1)))
    forward = (stream_ext[:, 2:], span_ext[:, :, 2:], padded[:, :, :, 2:])
    backward = (stream_ext[:, :-2], span_ext[:, :, :-2], padded[:, :, :, :-2])
    gradient = [[0.5 * (forward[index_b][index_a] - backward[index_b][index_a]) for index_b in range(3)] for index_a in range(3)]
    laplace = forward[0] + backward[0] + forward[1] + backward[1] + forward[2] + backward[2] - 6.0 * center
    strain_sq = jnp.zeros_like(center[0])
    for index_a in range(3):
        for index_b in range(3):
            sym_part = 0.5 * (gradient[index_a][index_b] + gradient[index_b][index_a])
            strain_sq = strain_sq + sym_part * sym_part
    eddy_visc = SMAGORINSKY * jnp.sqrt(2.0 * strain_sq + 1e-06)
    advection = jnp.stack([center[0] * gradient[index_a][0] + center[1] * gradient[index_a][1] + center[2] * gradient[index_a][2] for index_a in range(3)])
    return -advection + (VISCOSITY + eddy_visc) * laplace

def lorentz(center, magnet):
    aligned = lax.optimization_barrier(jnp.sum(center * magnet, axis=0))
    strength = lax.optimization_barrier(jnp.sum(magnet * magnet, axis=0))
    return INTERACTION * (aligned * magnet - strength * center)

def reference(main_flow, precursor, magnet_field, inlet_rows):
    inflow = jnp.take(precursor[:, -1], inlet_rows, axis=1)
    main_all = jnp.concatenate([inflow[:, None], main_flow, main_flow[:, -1:]], axis=1)

    def advance_main(block, result):
        offset = (block * CX).astype(jnp.int32)
        stream_ext = lax.dynamic_slice_in_dim(main_all, offset, CX + 2, 1)
        center = stream_ext[:, 1:-1]
        magnet = lax.dynamic_slice_in_dim(magnet_field, offset, CX, 1)
        span_ext = jnp.pad(center, ((0, 0), (0, 0), (1, 1), (0, 0)))
        updated = center + TIME_STEP * (tendency(center, stream_ext, span_ext) + lorentz(center, magnet))
        return lax.dynamic_update_slice_in_dim(result, updated, offset, 1)
    main_next = lax.fori_loop(0, NX // CX, advance_main, jnp.zeros_like(main_flow))
    prec_all = jnp.concatenate([precursor[:, -1:], precursor, precursor[:, :1]], axis=1)

    def advance_prec(block, result):
        offset = (block * PCX).astype(jnp.int32)
        stream_ext = lax.dynamic_slice_in_dim(prec_all, offset, PCX + 2, 1)
        center = stream_ext[:, 1:-1]
        span_ext = jnp.pad(center, ((0, 0), (0, 0), (1, 1), (0, 0)))
        updated = center + TIME_STEP * tendency(center, stream_ext, span_ext)
        return lax.dynamic_update_slice_in_dim(result, updated, offset, 1)
    precursor_next = lax.fori_loop(0, PX // PCX, advance_prec, jnp.zeros_like(precursor))
    return (main_next, precursor_next)
```

```python
import functools

import jax
import jax.numpy as jnp
from jax import lax
from jax.experimental import pallas as pl
from jax.experimental.pallas import tpu as pltpu
from jax.sharding import PartitionSpec as P

TIME_STEP = 0.1
VISCOSITY = 0.02
SMAGORINSKY = 0.03
INTERACTION = 0.5

LANES = 128
SUBLANES = 8
VMEM_LIMIT = 56 << 20
SMALL = pl.CostEstimate(flops=1, bytes_accessed=1, transcendentals=0)
F32 = jnp.float32
ANY = pl.BlockSpec(memory_space=pl.ANY)
HBM = pl.BlockSpec(memory_space=pltpu.HBM)
VMEM = pl.BlockSpec(memory_space=pltpu.VMEM)
SMEM = pl.BlockSpec(memory_space=pltpu.SMEM)

EDDY_SCALE = (TIME_STEP * SMAGORINSKY) ** 2 / 4.0
EDDY_FLOOR = (TIME_STEP * SMAGORINSKY) ** 2 * 1e-06


def update(u, forward, backward, magnet):
    diff = [[forward[j][i] - backward[j][i] for j in range(3)] for i in range(3)]
    diag = diff[0][0] * diff[0][0] + diff[1][1] * diff[1][1] + diff[2][2] * diff[2][2]
    quad = diag + diag
    for i, j in ((0, 1), (0, 2), (1, 2)):
        pair = diff[i][j] + diff[j][i]
        quad = quad + pair * pair
    square = quad * EDDY_SCALE + EDDY_FLOOR
    eddy = square * lax.rsqrt(square)
    visc = eddy + TIME_STEP * VISCOSITY
    keep = (1.0 - 6.0 * TIME_STEP * VISCOSITY) - 6.0 * eddy
    if magnet is not None:
        scale = TIME_STEP * INTERACTION
        aligned = (u[0] * magnet[0] + u[1] * magnet[1] + u[2] * magnet[2]) * scale
        strength = magnet[0] * magnet[0] + magnet[1] * magnet[1] + magnet[2] * magnet[2]
        keep = keep - strength * scale
    speed = [u[j] * (-0.5 * TIME_STEP) for j in range(3)]
    out = []
    for i in range(3):
        around = (forward[0][i] + backward[0][i]) + (forward[1][i] + backward[1][i])
        around = around + (forward[2][i] + backward[2][i])
        value = keep * u[i] + visc * around
        value = value + speed[0] * diff[i][0] + speed[1] * diff[i][1] + speed[2] * diff[i][2]
        if magnet is not None:
            value = value + aligned * magnet[i]
        out.append(value)
    return out


def shifted_lanes(read, tiles):
    shape = (SUBLANES, LANES)
    lane = lax.broadcasted_iota(jnp.int32, shape, 1)
    zero = jnp.zeros(shape, F32)
    here = read(0)
    left = zero
    ahead = pltpu.roll(here, LANES - 1, 1)
    for t in range(tiles):
        behind = pltpu.roll(here, 1, 1)
        following = read(t + 1) if t + 1 < tiles else None
        right = pltpu.roll(following, LANES - 1, 1) if t + 1 < tiles else zero
        yield here, jnp.where(lane == LANES - 1, right, ahead), jnp.where(lane == 0, left, behind)
        here, left, ahead = following, behind, right


def plane_rows(flow, before, x, after, at, magnet, store):
    tiles = flow.shape[2]
    streams = [
        shifted_lanes(lambda t, c=c: flow[c, x, t, pl.ds(at, SUBLANES), :], tiles) for c in range(3)
    ]
    for t in range(tiles):
        along = [next(stream) for stream in streams]
        u = [value[0] for value in along]
        forward = [
            [flow[c, after, t, pl.ds(at, SUBLANES), :] for c in range(3)],
            [flow[c, x, t, pl.ds(at + 1, SUBLANES), :] for c in range(3)],
            [value[1] for value in along],
        ]
        backward = [
            [flow[c, before, t, pl.ds(at, SUBLANES), :] for c in range(3)],
            [flow[c, x, t, pl.ds(at - 1, SUBLANES), :] for c in range(3)],
            [value[2] for value in along],
        ]
        field = None if magnet is None else [magnet(c, t) for c in range(3)]
        for c, value in enumerate(update(u, forward, backward, field)):
            store(c, t, value)


def tile_of(t):
    return pl.ds(t * LANES, LANES)


def place():
    span, stream = lax.axis_index("span"), lax.axis_index("stream")
    return span == 0, span == lax.axis_size("span") - 1, stream == 0, stream == lax.axis_size("stream") - 1


def copy_planes(source, first, count, flow, i, sem):
    for t in range(flow.shape[2]):
        pltpu.make_async_copy(
            source.at[:, pl.ds(first, count), :, tile_of(t)],
            flow.at[:, pl.ds(i, count), t, pl.ds(BASE, source.shape[2])],
            sem,
        ).start()


def wait_planes(flow, count, rows, sem):
    part = flow.at[:, pl.ds(0, count), :, pl.ds(BASE, rows)]
    pltpu.make_async_copy(part, part, sem).wait()


BASE = SUBLANES
GROUP = 4


def copy_halos(low, high, flow, i, first, count, rows, sem):
    walls = place()
    for n, (ref, at) in enumerate(((low, BASE - 1), (high, BASE + rows))):

        @pl.when(jnp.logical_not(walls[n]))
        def _(n=n, ref=ref, at=at):
            for t in range(flow.shape[2]):
                pltpu.make_async_copy(
                    ref.at[:, pl.ds(first, count), :, tile_of(t)],
                    flow.at[:, pl.ds(i, count), t, pl.ds(at, 1)],
                    sem.at[n],
                ).start()

        @pl.when(walls[n])
        def _(at=at):
            for c in range(3):
                for x in range(count):
                    for t in range(flow.shape[2]):
                        flow[c, i + x, t, pl.ds(at, 1), :] = jnp.zeros((1, LANES), F32)


def wait_halos(flow, i, count, rows, sem):
    walls = place()
    for n, at in enumerate((BASE - 1, BASE + rows)):

        @pl.when(jnp.logical_not(walls[n]))
        def _(n=n, at=at):
            part = flow.at[:, pl.ds(i, count), :, pl.ds(at, 1)]
            pltpu.make_async_copy(part, part, sem.at[n]).wait()


def interior_kernel(edges, n_main, n_prec, rows, *refs):
    if edges:
        main, prec, magnet, low, high, _, _, main_out, prec_out = refs[:9]
        flow, field, result, in_sem, field_sem, out_sem, halo_sem = refs[9:]
    else:
        main, prec, magnet, main_out, prec_out, token = refs[:6]
        flow, field, result, in_sem, field_sem, out_sem = refs[6:]
        token[...] = jnp.zeros_like(token)
    total = n_main + n_prec
    last = rows // SUBLANES - 1
    kept = [0, last] if edges else list(range(1, last))
    if edges:
        spans = [(0, 0, SUBLANES), (SUBLANES, last * SUBLANES, SUBLANES)]
    else:
        spans = [(0, SUBLANES, (last - 1) * SUBLANES)]

    if edges:
        copy_halos(low, high, flow, 0, 0, total, rows, halo_sem)
    for g in range(n_prec // GROUP):
        copy_planes(prec, g * GROUP, GROUP, flow, g * GROUP, in_sem.at[g])
    for g in range(n_main // GROUP):
        copy_planes(main, g * GROUP, GROUP, flow, n_prec + g * GROUP, in_sem.at[n_prec // GROUP + g])
        planes = pl.ds(g * GROUP, GROUP)
        for at, row, size in spans:
            pltpu.make_async_copy(
                magnet.at[:, planes, pl.ds(row, size)], field.at[:, planes, pl.ds(at, size)], field_sem.at[g]
            ).start()

    def stores(target, x, i):
        return [
            pltpu.make_async_copy(
                result.at[:, i, pl.ds(at, size)], target.at[:, x, pl.ds(row, size)], out_sem.at[i]
            )
            for at, row, size in spans
        ]

    def run(target, x, i, with_field):
        for n, k in enumerate(kept):
            part = pl.ds(n * SUBLANES, SUBLANES)

            def store(c, t, value, part=part):
                result[c, i, part, tile_of(t)] = value

            def read(c, t, part=part):
                return field[c, x, part, tile_of(t)]

            at = BASE + k * SUBLANES
            plane_rows(flow, i - 1, i, i + 1, at, read if with_field else None, store)
        for copy in stores(target, x, i):
            copy.start()

    def wait_field(g):
        part = field.at[:, pl.ds(0, GROUP)]
        pltpu.make_async_copy(part, part, field_sem.at[g]).wait()

    if edges:
        wait_halos(flow, 0, total, rows, halo_sem)
    wait_planes(flow, GROUP, rows, in_sem.at[0])

    def prec_step(x, carry):
        @pl.when((x + 1) % GROUP == 0)
        def _():
            wait_planes(flow, GROUP, rows, in_sem.at[(x + 1) // GROUP])

        run(prec_out, x, x, False)
        return carry

    lax.fori_loop(1, n_prec - 1, prec_step, 0)
    wait_planes(flow, GROUP, rows, in_sem.at[n_prec // GROUP])
    wait_field(0)

    def main_step(x, carry):
        @pl.when((x + 1) % GROUP == 0)
        def _():
            g = (x + 1) // GROUP
            wait_planes(flow, GROUP, rows, in_sem.at[n_prec // GROUP + g])
            wait_field(g)

        run(main_out, x, n_prec + x, True)
        return carry

    lax.fori_loop(1, n_main - 1, main_step, 0)

    def drain(i, carry):
        part = result.at[:, 0]
        pltpu.make_async_copy(part, part, out_sem.at[i]).wait()
        return carry

    lax.fori_loop(1, n_prec - 1, drain, 0)
    lax.fori_loop(n_prec + 1, total - 1, drain, 0)


def interior(edges, main, prec, magnet, extra=()):
    _, n_main, rows, depth = main.shape
    n_prec = prec.shape[1]
    total = n_main + n_prec
    kept = 2 * SUBLANES if edges else rows - 2 * SUBLANES
    scratch = [
        pltpu.VMEM((3, total, depth // LANES, rows + 2 * SUBLANES, LANES), F32),
        pltpu.VMEM((3, n_main, kept, depth), F32),
        pltpu.VMEM((3, total, kept, depth), F32),
        pltpu.SemaphoreType.DMA((total // GROUP,)),
        pltpu.SemaphoreType.DMA((n_main // GROUP,)),
        pltpu.SemaphoreType.DMA((total,)),
    ]
    outs = [jax.ShapeDtypeStruct(main.shape, F32), jax.ShapeDtypeStruct(prec.shape, F32)]
    out_specs = [HBM, HBM]
    if edges:
        scratch += [pltpu.SemaphoreType.DMA((2,))]
        low, high, main_out, prec_out = extra
        operands = (main, prec, magnet, low, high, main_out, prec_out)
        specs = [HBM] * 3 + [ANY] * 2 + [HBM] * 2
        aliases = {5: 0, 6: 1}
    else:
        operands = (main, prec, magnet)
        specs = [HBM] * 3
        aliases = {}
        outs.append(jax.ShapeDtypeStruct((SUBLANES, LANES), F32))
        out_specs.append(VMEM)
    return pl.pallas_call(
        functools.partial(interior_kernel, edges, n_main, n_prec, rows),
        out_shape=outs,
        in_specs=specs,
        out_specs=out_specs,
        scratch_shapes=scratch,
        input_output_aliases=aliases,
        compiler_params=pltpu.CompilerParams(vmem_limit_bytes=VMEM_LIMIT),
        cost_estimate=SMALL,
        name="edge_rows" if edges else "inner_rows",
    )(*operands)


def boundary_kernel(n_main, n_prec, rows, jobs, chunks, *refs):
    main, prec, magnet, low, high, before, after = refs[:7]
    slots = refs[7 : 7 + chunks]
    main_out, prec_out = refs[9 + chunks : 11 + chunks]
    flow, field, result, sem, side_sem, out_sem, halo_sem, field_sem = refs[11 + chunks :]
    last = rows // SUBLANES - 1
    tiles = flow.shape[2]
    _, _, at_inlet, at_outlet = place()
    half = lax.axis_index("span") % 2

    def fill(source, first, job, at):
        copy_planes(source, first, 1, flow, 3 * job + at, side_sem.at[job])

    for job, (is_main, at_low) in enumerate(jobs):
        source = main if is_main else prec
        count = n_main if is_main else n_prec
        kind = 0 if is_main else 1
        x = 0 if at_low else count - 1
        if at_low:
            copy_planes(source, 0, 2, flow, 3 * job + 1, sem.at[job])
        else:
            copy_planes(source, count - 2, 2, flow, 3 * job, sem.at[job])
        if is_main:
            pltpu.make_async_copy(magnet.at[:, x], field.at[:, job], field_sem.at[job]).start()
        copy_halos(low, high, flow, 3 * job + 1, n_prec + x if is_main else x, 1, rows, halo_sem.at[job])
        if at_low and is_main:

            @pl.when(at_inlet)
            def _(job=job):
                for k in range(chunks):
                    begin = jnp.bitwise_xor(half, k) * (tiles // chunks)
                    for t in range(tiles // chunks):
                        pltpu.make_async_copy(
                            slots[k].at[:, :, tile_of(t)],
                            flow.at[:, 3 * job, begin + t, pl.ds(BASE, rows)],
                            side_sem.at[job],
                        ).start()

            @pl.when(jnp.logical_not(at_inlet))
            def _(job=job, kind=kind):
                fill(before, kind, job, 0)

        elif at_low:
            fill(before, kind, job, 0)
        elif is_main:

            @pl.when(at_outlet)
            def _(job=job, source=source, x=x):
                fill(source, x, job, 2)

            @pl.when(jnp.logical_not(at_outlet))
            def _(job=job, kind=kind):
                fill(after, kind, job, 2)

        else:
            fill(after, kind, job, 2)
    for job, (is_main, at_low) in enumerate(jobs):
        x = 0 if at_low else (n_main if is_main else n_prec) - 1
        middle = 3 * job + 1
        wait_planes(flow, 2, rows, sem.at[job])
        wait_planes(flow, 1, rows, side_sem.at[job])
        wait_halos(flow, middle, 1, rows, halo_sem.at[job])
        if is_main:
            pltpu.make_async_copy(field.at[:, job], field.at[:, job], field_sem.at[job]).wait()

        def step(k, carry, job=job, middle=middle, is_main=is_main):
            part = pl.ds(pl.multiple_of(k * SUBLANES, SUBLANES), SUBLANES)

            def store(c, t, value):
                result[c, job, part, tile_of(t)] = value

            def read(c, t):
                return field[c, job, part, tile_of(t)]

            at = BASE + k * SUBLANES
            plane_rows(flow, middle - 1, middle, middle + 1, at, read if is_main else None, store)
            return carry

        lax.fori_loop(0, last + 1, step, 0, unroll=2)
        target = main_out if is_main else prec_out
        pltpu.make_async_copy(result.at[:, job], target.at[:, x], out_sem.at[job]).start()
    for job, (is_main, at_low) in enumerate(jobs):
        pltpu.make_async_copy(result.at[:, job], main_out.at[:, 0], out_sem.at[job]).wait()


def boundary(jobs, main, prec, magnet, low, high, before, after, slots, main_out, prec_out):
    _, n_main, rows, depth = main.shape
    n_prec = prec.shape[1]
    count = len(jobs)
    return pl.pallas_call(
        functools.partial(boundary_kernel, n_main, n_prec, rows, jobs, len(slots)),
        out_shape=[jax.ShapeDtypeStruct(main.shape, F32), jax.ShapeDtypeStruct(prec.shape, F32)],
        in_specs=[HBM] * 3 + [ANY] * (4 + len(slots)) + [HBM] * 2,
        out_specs=[HBM, HBM],
        scratch_shapes=[
            pltpu.VMEM((3, 3 * count, depth // LANES, rows + 2 * SUBLANES, LANES), F32),
            pltpu.VMEM((3, count, rows, depth), F32),
            pltpu.VMEM((3, count, rows, depth), F32),
            pltpu.SemaphoreType.DMA((count,)),
            pltpu.SemaphoreType.DMA((count,)),
            pltpu.SemaphoreType.DMA((count,)),
            pltpu.SemaphoreType.DMA((count, 2)),
            pltpu.SemaphoreType.DMA((count,)),
        ],
        input_output_aliases={7 + len(slots): 0, 8 + len(slots): 1},
        compiler_params=pltpu.CompilerParams(vmem_limit_bytes=VMEM_LIMIT),
        cost_estimate=SMALL,
        name="end_planes" if count > 1 else "inlet_plane",
    )(main, prec, magnet, low, high, before, after, *slots, main_out, prec_out)


def pack_kernel(n_main, n_prec, rows, depth, *refs):
    main, prec, row_low, row_high, face_low, face_high, kept, given, low_tile, high_tile, sem, row_sem = refs
    half = lax.axis_index("span") % 2
    width = depth // 2
    own = pl.ds(pl.multiple_of(half * width, width), width)
    other = pl.ds(pl.multiple_of((1 - half) * width, width), width)
    first, last = pl.ds(0, SUBLANES), pl.ds(rows - SUBLANES, SUBLANES)
    groups = [(prec, g, g) for g in range(0, n_prec, GROUP)] + [(main, g, n_prec + g) for g in range(0, n_main, GROUP)]
    row_copies = []
    for n, (source, x, i) in enumerate(groups):
        for m, (part, target) in enumerate(((first, low_tile), (last, high_tile))):
            row_copies.append(
                pltpu.make_async_copy(
                    source.at[:, pl.ds(x, GROUP), part], target.at[:, pl.ds(i, GROUP)], row_sem.at[2 * n + m]
                )
            )
    pairs = [
        (prec.at[:, n_prec - 1, :, other], given),
        (prec.at[:, n_prec - 1, :, own], kept),
    ]
    for source, kind, count in ((main, 0, n_main), (prec, 1, n_prec)):
        pairs.append((source.at[:, count - 1], face_high.at[:, kind]))
        pairs.append((source.at[:, 0], face_low.at[:, kind]))
    copies = [pltpu.make_async_copy(a, b, sem.at[n]) for n, (a, b) in enumerate(pairs)]
    for copy in row_copies + copies:
        copy.start()
    for n, (_, _, i) in enumerate(groups):
        row_copies[2 * n].wait()
        row_copies[2 * n + 1].wait()
        for c in range(3):
            for x in range(i, i + GROUP):
                row_low[c, x] = low_tile[c, x, pl.ds(0, 1), :]
                row_high[c, x] = high_tile[c, x, pl.ds(SUBLANES - 1, 1), :]
    for copy in copies:
        copy.wait()


def pack(main, prec):
    _, n_main, rows, depth = main.shape
    n_prec = prec.shape[1]
    total = n_main + n_prec
    face = jax.ShapeDtypeStruct((3, 2, rows, depth), F32)
    packed = jax.ShapeDtypeStruct((3, total, 1, depth), F32)
    part = jax.ShapeDtypeStruct((3, rows, depth // 2), F32)
    return pl.pallas_call(
        functools.partial(pack_kernel, n_main, n_prec, rows, depth),
        out_shape=[packed, packed, face, face, part, part],
        in_specs=[HBM, HBM],
        out_specs=[VMEM] * 6,
        scratch_shapes=[
            pltpu.VMEM((3, total, SUBLANES, depth), F32),
            pltpu.VMEM((3, total, SUBLANES, depth), F32),
            pltpu.SemaphoreType.DMA((6,)),
            pltpu.SemaphoreType.DMA((2 * total // GROUP,)),
        ],
        compiler_params=pltpu.CompilerParams(vmem_limit_bytes=VMEM_LIMIT),
        cost_estimate=SMALL,
        name="pack_halos",
    )(main, prec)


def join_kernel(kept, arrived, out, sem):
    @pl.when(place()[3])
    def _():
        copies = [pltpu.make_async_copy(a, out.at[n], sem.at[n]) for n, a in enumerate((kept, arrived))]
        for copy in copies:
            copy.start()
        for copy in copies:
            copy.wait()


def join(kept, arrived):
    return pl.pallas_call(
        join_kernel,
        out_shape=jax.ShapeDtypeStruct((2,) + kept.shape, F32),
        in_specs=[ANY, ANY],
        out_specs=VMEM,
        scratch_shapes=[pltpu.SemaphoreType.DMA((2,))],
        compiler_params=pltpu.CompilerParams(vmem_limit_bytes=16 << 20),
        cost_estimate=SMALL,
        name="join_halves",
    )(kept, arrived)


def relay_kernel(rows, *refs):
    order = refs[0]
    sources = refs[1:-7]
    outs = refs[-6:-4]
    held, laid, sem, out_sem = refs[-4:]
    span_index = lax.axis_index("span")
    tiles = held.shape[3]

    @pl.when(place()[3])
    def _():
        for m, source in enumerate(sources):
            for t in range(tiles):
                pltpu.make_async_copy(source.at[:, :, :, tile_of(t)], held.at[m, :, :, t], sem.at[m]).start()
        for m in range(len(sources)):
            pltpu.make_async_copy(held.at[m], held.at[m], sem.at[m]).wait()
        for k in range(2):
            base = jnp.bitwise_xor(span_index, k) * rows

            def step(r, carry, k=k, base=base):
                row = order[base + r]
                away = jnp.bitwise_xor(row // rows, span_index)
                at = row % rows
                for c in range(3):
                    for t in range(tiles):
                        laid[k, c, t, pl.ds(r, 1), :] = held[away // 2, away % 2, c, t, pl.ds(at, 1), :]
                return carry

            lax.fori_loop(0, rows, step, 0, unroll=4)
            for t in range(tiles):
                pltpu.make_async_copy(laid.at[k, :, t], outs[k].at[:, :, tile_of(t)], out_sem.at[k]).start()
        for k in range(2):
            pltpu.make_async_copy(laid.at[k], laid.at[k], out_sem.at[k]).wait()


def relay(order, sources, token):
    _, _, rows, width = sources[0].shape
    piece = jax.ShapeDtypeStruct((3, rows, width), F32)
    tiles = width // LANES
    return pl.pallas_call(
        functools.partial(relay_kernel, rows),
        out_shape=[piece] * 2,
        in_specs=[SMEM] + [ANY] * (len(sources) + 1),
        out_specs=[ANY] * 2,
        scratch_shapes=[
            pltpu.VMEM((len(sources), 2, 3, tiles, rows, LANES), F32),
            pltpu.VMEM((2, 3, tiles, rows, LANES), F32),
            pltpu.SemaphoreType.DMA((len(sources),)),
            pltpu.SemaphoreType.DMA((2,)),
        ],
        compiler_params=pltpu.CompilerParams(vmem_limit_bytes=VMEM_LIMIT),
        cost_estimate=SMALL,
        name="relay_rows",
    )(order, *sources, token)


def shards(main, prec, magnet, inlet_rows):
    spans = lax.axis_size("span")
    streams = lax.axis_size("stream")
    last = streams - 1
    row_low, row_high, face_low, face_high, kept, given = pack(main, prec)
    axes = ("stream", "span")

    def hop(value, source, target, k):
        return lax.ppermute(
            value, axes, [(source * spans + a, target * spans + (a ^ k)) for a in range(spans)]
        )

    arrived = hop(given, last, last, 1)
    up_span = [(i, (i + 1) % spans) for i in range(spans)]
    up_stream = [(i, (i + 1) % streams) for i in range(streams)]
    low = lax.ppermute(row_high, "span", up_span)
    high = lax.ppermute(row_low, "span", [(b, a) for a, b in up_span])
    joined = join(kept, arrived)
    sources = [joined] + [hop(joined, last, last, 2 * m) for m in range(1, spans // 2)]
    *outs, token = interior(False, main, prec, magnet)
    face_low, face_high, token = lax.optimization_barrier((face_low, face_high, token))
    laid = relay(inlet_rows, sources, token)
    slots = [hop(laid[k], last, 0, k) for k in range(2)]
    before = lax.ppermute(face_high, "stream", up_stream)
    after = lax.ppermute(face_low, "stream", [(b, a) for a, b in up_stream])
    outs = interior(True, main, prec, magnet, (low, high, *outs))
    outs = boundary(
        ((False, True), (False, False), (True, False)),
        main, prec, magnet, low, high, before, after, (), *outs,
    )
    outs = boundary(((True, True),), main, prec, magnet, low, high, before, after, slots, *outs)
    return tuple(outs)


def solution(mesh):
    placed = P(None, "stream", "span", None)
    return jax.shard_map(
        shards,
        mesh=mesh,
        in_specs=(placed, placed, placed, P()),
        out_specs=(placed, placed),
        check_vma=False,
    )
```

```python
import functools

import jax
import jax.numpy as jnp
from jax import lax
from jax.experimental import pallas as pl
from jax.experimental.pallas import tpu as pltpu
from jax.sharding import PartitionSpec as P

TIME_STEP = 0.1
VISCOSITY = 0.02
SMAGORINSKY = 0.03
INTERACTION = 0.5

LANES = 128
SUBLANES = 8


def cost(micros):
    return pl.CostEstimate(flops=0, bytes_accessed=int(micros * 3.7e6), transcendentals=0)


def in_hbm(value):
    return pltpu.with_memory_space_constraint(value, pltpu.HBM)


F32 = jnp.float32
ANY = pl.BlockSpec(memory_space=pl.ANY)
HBM = pl.BlockSpec(memory_space=pltpu.HBM)
VMEM = pl.BlockSpec(memory_space=pltpu.VMEM)
SMEM = pl.BlockSpec(memory_space=pltpu.SMEM)

EDDY_SCALE = (TIME_STEP * SMAGORINSKY) ** 2 / 4.0
EDDY_FLOOR = (TIME_STEP * SMAGORINSKY) ** 2 * 1e-06


def update(u, forward, backward, magnet):
    diff = [[forward[j][i] - backward[j][i] for j in range(3)] for i in range(3)]
    diag = diff[0][0] * diff[0][0] + diff[1][1] * diff[1][1] + diff[2][2] * diff[2][2]
    quad = diag + diag
    for i, j in ((0, 1), (0, 2), (1, 2)):
        pair = diff[i][j] + diff[j][i]
        quad = quad + pair * pair
    square = quad * EDDY_SCALE + EDDY_FLOOR
    eddy = square * lax.rsqrt(square)
    visc = eddy + TIME_STEP * VISCOSITY
    keep = (1.0 - 6.0 * TIME_STEP * VISCOSITY) - 6.0 * eddy
    if magnet is not None:
        scale = TIME_STEP * INTERACTION
        aligned = (u[0] * magnet[0] + u[1] * magnet[1] + u[2] * magnet[2]) * scale
        strength = magnet[0] * magnet[0] + magnet[1] * magnet[1] + magnet[2] * magnet[2]
        keep = keep - strength * scale
    speed = [u[j] * (-0.5 * TIME_STEP) for j in range(3)]
    out = []
    for i in range(3):
        around = (forward[0][i] + backward[0][i]) + (forward[1][i] + backward[1][i])
        around = around + (forward[2][i] + backward[2][i])
        value = keep * u[i] + visc * around
        value = value + speed[0] * diff[i][0] + speed[1] * diff[i][1] + speed[2] * diff[i][2]
        if magnet is not None:
            value = value + aligned * magnet[i]
        out.append(value)
    return out


def shifted_lanes(read, tiles):
    shape = (SUBLANES, LANES)
    lane = lax.broadcasted_iota(jnp.int32, shape, 1)
    zero = jnp.zeros(shape, F32)
    here = read(0)
    left = zero
    ahead = pltpu.roll(here, LANES - 1, 1)
    for t in range(tiles):
        behind = pltpu.roll(here, 1, 1)
        following = read(t + 1) if t + 1 < tiles else None
        right = pltpu.roll(following, LANES - 1, 1) if t + 1 < tiles else zero
        yield here, jnp.where(lane == LANES - 1, right, ahead), jnp.where(lane == 0, left, behind)
        here, left, ahead = following, behind, right


def plane_rows(center, low, high, before, after, magnet, store, tiles):
    streams = [shifted_lanes(lambda t, c=c: center(c, t), tiles) for c in range(3)]
    for t in range(tiles):
        along = [next(stream) for stream in streams]
        u = [value[0] for value in along]
        forward = [
            [after(c, t) for c in range(3)],
            [high(c, t) for c in range(3)],
            [value[1] for value in along],
        ]
        backward = [
            [before(c, t) for c in range(3)],
            [low(c, t) for c in range(3)],
            [value[2] for value in along],
        ]
        field = None if magnet is None else [magnet(c, t) for c in range(3)]
        for c, value in enumerate(update(u, forward, backward, field)):
            store(c, t, value)


BASE = SUBLANES
GROUP = 4


def tile_of(t):
    return pl.ds(t * LANES, LANES)


def rows_of(ref, x, at):
    return lambda c, t: ref[c, x, t, pl.ds(at, SUBLANES), :]


def span_of(ref, x, at):
    return lambda c, t: ref[c, x, pl.ds(at, SUBLANES), tile_of(t)]


def span_rows(ref, c, t, k):
    return ref[c, pl.ds(k * SUBLANES, SUBLANES), tile_of(t)]


def with_row(inside, halo, x, edge):
    def read(c, t):
        sub = lax.broadcasted_iota(jnp.int32, (SUBLANES, LANES), 0)
        row = jnp.broadcast_to(halo[c, x, :, tile_of(t)], (SUBLANES, LANES))
        return jnp.where(sub == edge, row, inside(c, t))

    return read


def edge_of(flow, low, high, x, k, last):
    at = BASE + k * SUBLANES
    below, above = rows_of(flow, x, at - 1), rows_of(flow, x, at + 1)
    if k == 0:
        below = with_row(below, low, x, 0)
    if k == last:
        above = with_row(above, high, x, SUBLANES - 1)
    return below, above


def place():
    span, stream = lax.axis_index("span"), lax.axis_index("stream")
    return span == 0, span == lax.axis_size("span") - 1, stream == 0, stream == lax.axis_size("stream") - 1


def wait_part(part, sem):
    pltpu.make_async_copy(part, part, sem).wait()


def interior_kernel(edges, n_main, n_prec, rows, *refs):
    if edges:
        flow, magnet, low, high, _, _, main_out, prec_out, field, result, field_sem, out_sem = refs
    else:
        main, prec, magnet, main_out, prec_out, flow, face_low, face_high = refs[:8]
        field, result, field_sem, out_sem, in_sem, face_sem = refs[8:]
    tiles = flow.shape[2]
    total = n_main + n_prec
    last = rows // SUBLANES - 1
    kept = [0, last] if edges else list(range(1, last))
    if edges:
        spans = [(0, 0, SUBLANES), (SUBLANES, last * SUBLANES, SUBLANES)]
    else:
        spans = [(0, SUBLANES, (last - 1) * SUBLANES)]

    def load(source, x, i):
        for t in range(tiles):
            pltpu.make_async_copy(
                source.at[:, pl.ds(x, GROUP), :, tile_of(t)],
                flow.at[:, pl.ds(i, GROUP), t, pl.ds(BASE, rows)],
                in_sem.at[i // GROUP],
            ).start()

    def load_field(x):
        for at, row, size in spans:
            pltpu.make_async_copy(
                magnet.at[:, pl.ds(x, GROUP), pl.ds(row, size)],
                field.at[:, pl.ds(x, GROUP), pl.ds(at, size)],
                field_sem.at[x // GROUP],
            ).start()

    def wait_flow(g):
        if not edges:
            wait_part(flow.at[:, pl.ds(0, GROUP), :, pl.ds(BASE, rows)], in_sem.at[g])

    def wait_field(g):
        wait_part(field.at[:, pl.ds(0, GROUP)], field_sem.at[g])

    if not edges:
        for x in range(0, n_prec, GROUP):
            load(prec, x, x)
    for x in range(0, n_main, GROUP):
        if not edges:
            load(main, x, n_prec + x)
        load_field(x)
    faces = []
    if not edges:
        for kind, source, count in ((0, main, n_main), (1, prec, n_prec)):
            faces.append((source.at[:, 0], face_low.at[:, kind]))
            faces.append((source.at[:, count - 1], face_high.at[:, kind]))
        faces = [pltpu.make_async_copy(a, b, face_sem.at[n]) for n, (a, b) in enumerate(faces)]
        for copy in faces:
            copy.start()

    def run(target, x, i, with_field):
        for n, k in enumerate(kept):
            at = BASE + k * SUBLANES

            def store(c, t, value, n=n):
                result[c, i, pl.ds(n * SUBLANES, SUBLANES), tile_of(t)] = value

            if edges:
                below, above = edge_of(flow, low, high, i, k, last)
            else:
                below, above = rows_of(flow, i, at - 1), rows_of(flow, i, at + 1)
            plane_rows(
                rows_of(flow, i, at),
                below,
                above,
                rows_of(flow, i - 1, at),
                rows_of(flow, i + 1, at),
                span_of(field, x, n * SUBLANES) if with_field else None,
                store,
                tiles,
            )
        for at, row, size in spans:
            pltpu.make_async_copy(
                result.at[:, i, pl.ds(at, size)], target.at[:, x, pl.ds(row, size)], out_sem.at[i]
            ).start()

    wait_flow(0)

    def prec_step(x, carry):
        @pl.when((x + 1) % GROUP == 0)
        def _():
            wait_flow((x + 1) // GROUP)

        run(prec_out, x, x, False)
        return carry

    lax.fori_loop(1, n_prec - 1, prec_step, 0)
    wait_flow(n_prec // GROUP)
    wait_field(0)

    def main_step(x, carry):
        @pl.when((x + 1) % GROUP == 0)
        def _():
            wait_flow((n_prec + x + 1) // GROUP)
            wait_field((x + 1) // GROUP)

        run(main_out, x, n_prec + x, True)
        return carry

    lax.fori_loop(1, n_main - 1, main_step, 0)
    for copy in faces:
        copy.wait()

    def drain(i, carry):
        wait_part(result.at[:, 0], out_sem.at[i])
        return carry

    lax.fori_loop(1, n_prec - 1, drain, 0)
    lax.fori_loop(n_prec + 1, total - 1, drain, 0)


def interior(edges, main_shape, prec_shape, operands):
    _, n_main, rows, depth = main_shape
    n_prec = prec_shape[1]
    total = n_main + n_prec
    kept = 2 * SUBLANES if edges else rows - 2 * SUBLANES
    scratch = [
        pltpu.VMEM((3, n_main, kept, depth), F32),
        pltpu.VMEM((3, total, kept, depth), F32),
        pltpu.SemaphoreType.DMA((n_main // GROUP,)),
        pltpu.SemaphoreType.DMA((total,)),
    ]
    outs = [jax.ShapeDtypeStruct(main_shape, F32), jax.ShapeDtypeStruct(prec_shape, F32)]
    out_specs = [HBM, HBM]
    if edges:
        specs = [VMEM, HBM, VMEM, VMEM, HBM, HBM]
        aliases = {4: 0, 5: 1}
    else:
        specs = [HBM] * 3
        aliases = {}
        scratch += [pltpu.SemaphoreType.DMA((total // GROUP,)), pltpu.SemaphoreType.DMA((4,))]
        outs.append(pltpu.VMEM((3, total, depth // LANES, rows + 2 * SUBLANES, LANES), F32))
        outs += [pltpu.VMEM((3, 2, rows, depth), F32)] * 2
        out_specs += [VMEM] * 3
    return pl.pallas_call(
        functools.partial(interior_kernel, edges, n_main, n_prec, rows),
        out_shape=outs,
        in_specs=specs,
        out_specs=out_specs,
        scratch_shapes=scratch,
        input_output_aliases=aliases,
        compiler_params=pltpu.CompilerParams(vmem_limit_bytes=16 << 20),
        cost_estimate=cost(8 if edges else 9),
        name="edge_rows" if edges else "inner_rows",
    )(*operands)


def boundary_kernel(n_main, n_prec, rows, jobs, chunks, *refs):
    flow, magnet, low, high, before, after = refs[:6]
    slots = refs[6 : 6 + chunks]
    main_out, prec_out, field, result, field_sem, out_sem = refs[8 + chunks :]
    last = rows // SUBLANES - 1
    tiles = flow.shape[2]
    _, _, at_inlet, at_outlet = place()
    for job, (is_main, at_low) in enumerate(jobs):
        if is_main:
            x = 0 if at_low else n_main - 1
            pltpu.make_async_copy(magnet.at[:, x], field.at[:, job], field_sem.at[job]).start()
    for job, (is_main, at_low) in enumerate(jobs):
        x = 0 if at_low else (n_main if is_main else n_prec) - 1
        i = n_prec + x if is_main else x
        if is_main:
            wait_part(field.at[:, job], field_sem.at[job])
        for k in range(last + 1):
            at = BASE + k * SUBLANES
            center = rows_of(flow, i, at)
            face = span_of(before if at_low else after, 0 if is_main else 1, k * SUBLANES)

            def store(c, t, value, job=job, k=k):
                result[c, job, pl.ds(k * SUBLANES, SUBLANES), tile_of(t)] = value

            def inlet(c, t, k=k, face=face):
                fed = span_rows(slots[0], c, t, k) + span_rows(slots[1], c, t, k)
                return jnp.where(at_inlet, fed, face(c, t))

            def outlet(c, t, center=center, face=face):
                return jnp.where(at_outlet, center(c, t), face(c, t))

            if is_main:
                face_side = inlet if at_low else outlet
            else:
                face_side = face
            below, above = edge_of(flow, low, high, i, k, last)
            plane_rows(
                center,
                below,
                above,
                face_side if at_low else rows_of(flow, i - 1, at),
                rows_of(flow, i + 1, at) if at_low else face_side,
                span_of(field, job, k * SUBLANES) if is_main else None,
                store,
                tiles,
            )
        target = main_out if is_main else prec_out
        pltpu.make_async_copy(result.at[:, job], target.at[:, x], out_sem.at[job]).start()
    for job in range(len(jobs)):
        wait_part(result.at[:, job], out_sem.at[job])


def boundary(jobs, n_main, n_prec, flow, magnet, low, high, before, after, slots, main_out, prec_out):
    _, _, rows, depth = magnet.shape
    count = len(jobs)
    chunks = len(slots)
    return pl.pallas_call(
        functools.partial(boundary_kernel, n_main, n_prec, rows, jobs, chunks),
        out_shape=[jax.ShapeDtypeStruct(main_out.shape, F32), jax.ShapeDtypeStruct(prec_out.shape, F32)],
        in_specs=[VMEM, HBM] + [VMEM] * (4 + chunks) + [HBM] * 2,
        out_specs=[HBM, HBM],
        scratch_shapes=[
            pltpu.VMEM((3, count, rows, depth), F32),
            pltpu.VMEM((3, count, rows, depth), F32),
            pltpu.SemaphoreType.DMA((count,)),
            pltpu.SemaphoreType.DMA((count,)),
        ],
        input_output_aliases={6 + chunks: 0, 7 + chunks: 1},
        compiler_params=pltpu.CompilerParams(vmem_limit_bytes=8 << 20),
        cost_estimate=cost(len(jobs)),
        name="end_planes",
    )(flow, magnet, low, high, before, after, *slots, main_out, prec_out)


def outlet_kernel(prec, plane, sem):
    copy = pltpu.make_async_copy(prec.at[:, prec.shape[1] - 1], plane, sem)
    copy.start()
    copy.wait()


def outlet(prec):
    _, _, rows, depth = prec.shape
    return pl.pallas_call(
        outlet_kernel,
        out_shape=pltpu.VMEM((3, rows, depth), F32),
        in_specs=[HBM],
        out_specs=VMEM,
        scratch_shapes=[pltpu.SemaphoreType.DMA],
        compiler_params=pltpu.CompilerParams(vmem_limit_bytes=2 << 20),
        cost_estimate=cost(1),
        name="outlet_plane",
    )(prec)


def pack_kernel(n_main, n_prec, rows, *refs):
    main, prec, row_low, row_high, low_tile, high_tile, sem = refs
    first, last = pl.ds(0, SUBLANES), pl.ds(rows - SUBLANES, SUBLANES)
    groups = [(prec, g, g) for g in range(0, n_prec, GROUP)] + [(main, g, n_prec + g) for g in range(0, n_main, GROUP)]
    copies = []
    for n, (source, x, i) in enumerate(groups):
        for m, (part, target) in enumerate(((first, low_tile), (last, high_tile))):
            copies.append(
                pltpu.make_async_copy(
                    source.at[:, pl.ds(x, GROUP), part], target.at[:, pl.ds(i, GROUP)], sem.at[2 * n + m]
                )
            )
    for copy in copies:
        copy.start()
    low_wall, high_wall, _, _ = place()
    for n, (_, _, i) in enumerate(groups):
        copies[2 * n].wait()
        copies[2 * n + 1].wait()
        for c in range(3):
            for x in range(i, i + GROUP):
                row_low[c, x] = low_tile[c, x, pl.ds(0, 1), :]
                row_high[c, x] = high_tile[c, x, pl.ds(SUBLANES - 1, 1), :]

    @pl.when(low_wall)
    def _():
        row_low[...] = jnp.zeros_like(row_low)

    @pl.when(high_wall)
    def _():
        row_high[...] = jnp.zeros_like(row_high)


def pack(main, prec):
    _, n_main, rows, depth = main.shape
    n_prec = prec.shape[1]
    total = n_main + n_prec
    packed = pltpu.VMEM((3, total, 1, depth), F32)
    return pl.pallas_call(
        functools.partial(pack_kernel, n_main, n_prec, rows),
        out_shape=[packed, packed],
        in_specs=[HBM, HBM],
        out_specs=[VMEM] * 2,
        scratch_shapes=[
            pltpu.VMEM((3, total, SUBLANES, depth), F32),
            pltpu.VMEM((3, total, SUBLANES, depth), F32),
            pltpu.SemaphoreType.DMA((2 * total // GROUP,)),
        ],
        compiler_params=pltpu.CompilerParams(vmem_limit_bytes=12 << 20),
        cost_estimate=cost(3),
        name="pack_rows",
    )(main, prec)


def relay_kernel(rows, *refs):
    order = refs[0]
    sources = refs[1:-6]
    outs = refs[-6:-4]
    held, laid, sem, out_sem = refs[-4:]
    span_index = lax.axis_index("span")
    tiles = held.shape[2]

    @pl.when(lax.axis_index("stream") == lax.axis_size("stream") - 2)
    def _():
        for m, source in enumerate(sources):
            for t in range(tiles):
                pltpu.make_async_copy(source.at[:, :, tile_of(t)], held.at[m, :, t], sem.at[m]).start()
        laid[...] = jnp.zeros_like(laid)
        for m in range(len(sources)):
            wait_part(held.at[m], sem.at[m])
        for k in range(2):
            base = jnp.bitwise_xor(span_index, k) * rows

            def step(r, carry, k=k, base=base):
                row = order[base + r]
                away = jnp.bitwise_xor(row // rows, span_index)
                at = row % rows

                @pl.when(away % 2 == 0)
                def _():
                    for c in range(3):
                        for t in range(tiles):
                            laid[k, c, t, pl.ds(r, 1), :] = held[away // 2, c, t, pl.ds(at, 1), :]

                return carry

            lax.fori_loop(0, rows, step, 0)
            for t in range(tiles):
                pltpu.make_async_copy(laid.at[k, :, t], outs[k].at[:, :, tile_of(t)], out_sem.at[k]).start()
        for k in range(2):
            wait_part(laid.at[k], out_sem.at[k])


def relay(order, sources):
    _, rows, depth = sources[0].shape
    piece = pltpu.VMEM((3, rows, depth), F32)
    tiles = depth // LANES
    return pl.pallas_call(
        functools.partial(relay_kernel, rows),
        out_shape=[piece] * 2,
        in_specs=[SMEM] + [VMEM] * len(sources),
        out_specs=[VMEM] * 2,
        scratch_shapes=[
            pltpu.VMEM((len(sources), 3, tiles, rows, LANES), F32),
            pltpu.VMEM((2, 3, tiles, rows, LANES), F32),
            pltpu.SemaphoreType.DMA((len(sources),)),
            pltpu.SemaphoreType.DMA((2,)),
        ],
        compiler_params=pltpu.CompilerParams(vmem_limit_bytes=8 << 20),
        cost_estimate=cost(1),
        name="relay_rows",
    )(order, *sources)


def shards(main, prec, magnet, inlet_rows):
    spans = lax.axis_size("span")
    streams = lax.axis_size("stream")
    last = streams - 1
    n_main, n_prec = main.shape[1], prec.shape[1]
    main, prec, magnet = in_hbm(main), in_hbm(prec), in_hbm(magnet)
    axes = ("stream", "span")

    def hop(value, source, target, k):
        return lax.ppermute(
            value, axes, [(source * spans + a, target * spans + (a ^ k)) for a in range(spans)]
        )

    plane = outlet(prec)
    sources = [hop(plane, last, last - 1, 2 * m) for m in range(spans // 2)]
    row_low, row_high = pack(main, prec)
    row_low, row_high, sources[0] = lax.optimization_barrier((row_low, row_high, sources[0]))
    up_span = [(i, (i + 1) % spans) for i in range(spans)]
    up_stream = [(i, (i + 1) % streams) for i in range(streams)]
    low = lax.ppermute(row_high, "span", up_span)
    high = lax.ppermute(row_low, "span", [(b, a) for a, b in up_span])
    *outs, flow, face_low, face_high = interior(False, main.shape, prec.shape, (main, prec, magnet))
    face_low, face_high, low, high, *sources = lax.optimization_barrier((face_low, face_high, low, high, *sources))
    before = lax.ppermute(face_high, "stream", up_stream)
    after = lax.ppermute(face_low, "stream", [(b, a) for a, b in up_stream])
    laid = relay(inlet_rows, sources)
    slots = [hop(laid[k], last - 1, 0, k) for k in range(2)]
    outs = interior(True, main.shape, prec.shape, (flow, magnet, low, high, *outs))
    ends = ((False, True), (False, False), (True, False), (True, True))
    outs = boundary(ends, n_main, n_prec, flow, magnet, low, high, before, after, slots, *outs)
    return tuple(outs)


def solution(mesh):
    placed = P(None, "stream", "span", None)
    return jax.shard_map(
        shards,
        mesh=mesh,
        in_specs=(placed, placed, placed, P()),
        out_specs=(placed, placed),
        check_vma=False,
    )
```

```python
import functools

import jax
import jax.numpy as jnp
from jax import lax
from jax.experimental import pallas as pl
from jax.experimental.pallas import tpu as pltpu
from jax.sharding import PartitionSpec as P

TIME_STEP = 0.1
VISCOSITY = 0.02
SMAGORINSKY = 0.03
INTERACTION = 0.5

LANES = 128
SUBLANES = 8


def cost(micros):
    return pl.CostEstimate(flops=0, bytes_accessed=int(micros * 3.7e6), transcendentals=0)


def in_hbm(value):
    return pltpu.with_memory_space_constraint(value, pltpu.HBM)


F32 = jnp.float32
ANY = pl.BlockSpec(memory_space=pl.ANY)
HBM = pl.BlockSpec(memory_space=pltpu.HBM)
VMEM = pl.BlockSpec(memory_space=pltpu.VMEM)
SMEM = pl.BlockSpec(memory_space=pltpu.SMEM)

EDDY_SCALE = (TIME_STEP * SMAGORINSKY) ** 2 / 4.0
EDDY_FLOOR = (TIME_STEP * SMAGORINSKY) ** 2 * 1e-06


def update(u, forward, backward, magnet):
    diff = [[forward[j][i] - backward[j][i] for j in range(3)] for i in range(3)]
    diag = diff[0][0] * diff[0][0] + diff[1][1] * diff[1][1] + diff[2][2] * diff[2][2]
    quad = diag + diag
    for i, j in ((0, 1), (0, 2), (1, 2)):
        pair = diff[i][j] + diff[j][i]
        quad = quad + pair * pair
    square = quad * EDDY_SCALE + EDDY_FLOOR
    eddy = square * lax.rsqrt(square)
    visc = eddy + TIME_STEP * VISCOSITY
    keep = (1.0 - 6.0 * TIME_STEP * VISCOSITY) - 6.0 * eddy
    if magnet is not None:
        scale = TIME_STEP * INTERACTION
        aligned = (u[0] * magnet[0] + u[1] * magnet[1] + u[2] * magnet[2]) * scale
        strength = magnet[0] * magnet[0] + magnet[1] * magnet[1] + magnet[2] * magnet[2]
        keep = keep - strength * scale
    speed = [u[j] * (-0.5 * TIME_STEP) for j in range(3)]
    out = []
    for i in range(3):
        around = (forward[0][i] + backward[0][i]) + (forward[1][i] + backward[1][i])
        around = around + (forward[2][i] + backward[2][i])
        value = keep * u[i] + visc * around
        value = value + speed[0] * diff[i][0] + speed[1] * diff[i][1] + speed[2] * diff[i][2]
        if magnet is not None:
            value = value + aligned * magnet[i]
        out.append(value)
    return out


def shifted_lanes(read, tiles):
    shape = (SUBLANES, LANES)
    lane = lax.broadcasted_iota(jnp.int32, shape, 1)
    zero = jnp.zeros(shape, F32)
    here = read(0)
    left = zero
    ahead = pltpu.roll(here, LANES - 1, 1)
    for t in range(tiles):
        behind = pltpu.roll(here, 1, 1)
        following = read(t + 1) if t + 1 < tiles else None
        right = pltpu.roll(following, LANES - 1, 1) if t + 1 < tiles else zero
        yield here, jnp.where(lane == LANES - 1, right, ahead), jnp.where(lane == 0, left, behind)
        here, left, ahead = following, behind, right


def plane_rows(center, low, high, before, after, magnet, store, tiles):
    streams = [shifted_lanes(lambda t, c=c: center(c, t), tiles) for c in range(3)]
    for t in range(tiles):
        along = [next(stream) for stream in streams]
        u = [value[0] for value in along]
        forward = [
            [after(c, t) for c in range(3)],
            [high(c, t) for c in range(3)],
            [value[1] for value in along],
        ]
        backward = [
            [before(c, t) for c in range(3)],
            [low(c, t) for c in range(3)],
            [value[2] for value in along],
        ]
        field = None if magnet is None else [magnet(c, t) for c in range(3)]
        for c, value in enumerate(update(u, forward, backward, field)):
            store(c, t, value)


BASE = SUBLANES
GROUP = 4


def tile_of(t):
    return pl.ds(t * LANES, LANES)


def rows_of(ref, x, at):
    return lambda c, t: ref[c, x, t, pl.ds(at, SUBLANES), :]


def span_of(ref, x, at):
    return lambda c, t: ref[c, x, pl.ds(at, SUBLANES), tile_of(t)]


def span_rows(ref, c, t, k):
    return ref[c, pl.ds(k * SUBLANES, SUBLANES), tile_of(t)]


def with_row(inside, halo, x, edge):
    def read(c, t):
        sub = lax.broadcasted_iota(jnp.int32, (SUBLANES, LANES), 0)
        row = jnp.broadcast_to(halo[c, x, :, tile_of(t)], (SUBLANES, LANES))
        return jnp.where(sub == edge, row, inside(c, t))

    return read


def edge_of(flow, low, high, x, k, last):
    at = BASE + k * SUBLANES
    below, above = rows_of(flow, x, at - 1), rows_of(flow, x, at + 1)
    if k == 0:
        below = with_row(below, low, x, 0)
    if k == last:
        above = with_row(above, high, x, SUBLANES - 1)
    return below, above


def place():
    span, stream = lax.axis_index("span"), lax.axis_index("stream")
    return span == 0, span == lax.axis_size("span") - 1, stream == 0, stream == lax.axis_size("stream") - 1


def wait_part(part, sem):
    pltpu.make_async_copy(part, part, sem).wait()


def interior_kernel(edges, n_main, n_prec, rows, *refs):
    if edges:
        flow, magnet, low, high, _, _, main_out, prec_out, field, result, field_sem, out_sem = refs
    else:
        main, prec, magnet, main_out, prec_out, flow, face_low, face_high = refs[:8]
        field, result, field_sem, out_sem, in_sem, face_sem = refs[8:]
    tiles = flow.shape[2]
    total = n_main + n_prec
    last = rows // SUBLANES - 1
    kept = [0, last] if edges else list(range(1, last))
    if edges:
        spans = [(0, 0, SUBLANES), (SUBLANES, last * SUBLANES, SUBLANES)]
    else:
        spans = [(0, SUBLANES, (last - 1) * SUBLANES)]

    def load(source, x, i):
        for t in range(tiles):
            pltpu.make_async_copy(
                source.at[:, pl.ds(x, GROUP), :, tile_of(t)],
                flow.at[:, pl.ds(i, GROUP), t, pl.ds(BASE, rows)],
                in_sem.at[i // GROUP],
            ).start()

    def load_field(x):
        for at, row, size in spans:
            pltpu.make_async_copy(
                magnet.at[:, pl.ds(x, GROUP), pl.ds(row, size)],
                field.at[:, pl.ds(x, GROUP), pl.ds(at, size)],
                field_sem.at[x // GROUP],
            ).start()

    def wait_flow(g):
        if not edges:
            wait_part(flow.at[:, pl.ds(0, GROUP), :, pl.ds(BASE, rows)], in_sem.at[g])

    def wait_field(g):
        wait_part(field.at[:, pl.ds(0, GROUP)], field_sem.at[g])

    if not edges:
        for x in range(0, n_prec, GROUP):
            load(prec, x, x)
    for x in range(0, n_main, GROUP):
        if not edges:
            load(main, x, n_prec + x)
        load_field(x)
    faces = []
    if not edges:
        for kind, source, count in ((0, main, n_main), (1, prec, n_prec)):
            faces.append((source.at[:, 0], face_low.at[:, kind]))
            faces.append((source.at[:, count - 1], face_high.at[:, kind]))
        faces = [pltpu.make_async_copy(a, b, face_sem.at[n]) for n, (a, b) in enumerate(faces)]
        for copy in faces:
            copy.start()

    def run(target, x, i, with_field):
        for n, k in enumerate(kept):
            at = BASE + k * SUBLANES

            def store(c, t, value, n=n):
                result[c, i, pl.ds(n * SUBLANES, SUBLANES), tile_of(t)] = value

            if edges:
                below, above = edge_of(flow, low, high, i, k, last)
            else:
                below, above = rows_of(flow, i, at - 1), rows_of(flow, i, at + 1)
            plane_rows(
                rows_of(flow, i, at),
                below,
                above,
                rows_of(flow, i - 1, at),
                rows_of(flow, i + 1, at),
                span_of(field, x, n * SUBLANES) if with_field else None,
                store,
                tiles,
            )
        for at, row, size in spans:
            pltpu.make_async_copy(
                result.at[:, i, pl.ds(at, size)], target.at[:, x, pl.ds(row, size)], out_sem.at[i]
            ).start()

    wait_flow(0)

    def prec_step(x, carry):
        @pl.when((x + 1) % GROUP == 0)
        def _():
            wait_flow((x + 1) // GROUP)

        run(prec_out, x, x, False)
        return carry

    lax.fori_loop(1, n_prec - 1, prec_step, 0)
    wait_flow(n_prec // GROUP)
    wait_field(0)

    def main_step(x, carry):
        @pl.when((x + 1) % GROUP == 0)
        def _():
            wait_flow((n_prec + x + 1) // GROUP)
            wait_field((x + 1) // GROUP)

        run(main_out, x, n_prec + x, True)
        return carry

    lax.fori_loop(1, n_main - 1, main_step, 0)
    for copy in faces:
        copy.wait()

    def drain(i, carry):
        wait_part(result.at[:, 0], out_sem.at[i])
        return carry

    lax.fori_loop(1, n_prec - 1, drain, 0)
    lax.fori_loop(n_prec + 1, total - 1, drain, 0)


def interior(edges, main_shape, prec_shape, operands):
    _, n_main, rows, depth = main_shape
    n_prec = prec_shape[1]
    total = n_main + n_prec
    kept = 2 * SUBLANES if edges else rows - 2 * SUBLANES
    scratch = [
        pltpu.VMEM((3, n_main, kept, depth), F32),
        pltpu.VMEM((3, total, kept, depth), F32),
        pltpu.SemaphoreType.DMA((n_main // GROUP,)),
        pltpu.SemaphoreType.DMA((total,)),
    ]
    outs = [jax.ShapeDtypeStruct(main_shape, F32), jax.ShapeDtypeStruct(prec_shape, F32)]
    out_specs = [HBM, HBM]
    if edges:
        specs = [VMEM, HBM, VMEM, VMEM, HBM, HBM]
        aliases = {4: 0, 5: 1}
    else:
        specs = [HBM] * 3
        aliases = {}
        scratch += [pltpu.SemaphoreType.DMA((total // GROUP,)), pltpu.SemaphoreType.DMA((4,))]
        outs.append(pltpu.VMEM((3, total, depth // LANES, rows + 2 * SUBLANES, LANES), F32))
        outs += [pltpu.VMEM((3, 2, rows, depth), F32)] * 2
        out_specs += [VMEM] * 3
    return pl.pallas_call(
        functools.partial(interior_kernel, edges, n_main, n_prec, rows),
        out_shape=outs,
        in_specs=specs,
        out_specs=out_specs,
        scratch_shapes=scratch,
        input_output_aliases=aliases,
        compiler_params=pltpu.CompilerParams(vmem_limit_bytes=16 << 20),
        cost_estimate=cost(8 if edges else 9),
        name="edge_rows" if edges else "inner_rows",
    )(*operands)


def boundary_kernel(n_main, n_prec, rows, jobs, *refs):
    flow, magnet, low, high, before, after, fed = refs[:7]
    main_out, prec_out, field, result, field_sem, out_sem = refs[9:]
    last = rows // SUBLANES - 1
    tiles = flow.shape[2]
    at_outlet = place()[3]
    for job, (is_main, at_low) in enumerate(jobs):
        if is_main:
            x = 0 if at_low else n_main - 1
            pltpu.make_async_copy(magnet.at[:, x], field.at[:, job], field_sem.at[job]).start()
    for job, (is_main, at_low) in enumerate(jobs):
        x = 0 if at_low else (n_main if is_main else n_prec) - 1
        i = n_prec + x if is_main else x
        if is_main:
            wait_part(field.at[:, job], field_sem.at[job])
        for k in range(last + 1):
            at = BASE + k * SUBLANES
            center = rows_of(flow, i, at)
            face = span_of(before if at_low else after, 0 if is_main else 1, k * SUBLANES)

            def store(c, t, value, job=job, k=k):
                result[c, job, pl.ds(k * SUBLANES, SUBLANES), tile_of(t)] = value

            def inlet(c, t, k=k, face=face):
                return face(c, t) + span_rows(fed, c, t, k)

            def outlet(c, t, center=center, face=face):
                return jnp.where(at_outlet, center(c, t), face(c, t))

            if is_main:
                face_side = inlet if at_low else outlet
            else:
                face_side = face
            below, above = edge_of(flow, low, high, i, k, last)
            plane_rows(
                center,
                below,
                above,
                face_side if at_low else rows_of(flow, i - 1, at),
                rows_of(flow, i + 1, at) if at_low else face_side,
                span_of(field, job, k * SUBLANES) if is_main else None,
                store,
                tiles,
            )
        target = main_out if is_main else prec_out
        pltpu.make_async_copy(result.at[:, job], target.at[:, x], out_sem.at[job]).start()
    for job in range(len(jobs)):
        wait_part(result.at[:, job], out_sem.at[job])


def boundary(jobs, n_main, n_prec, flow, magnet, low, high, before, after, fed, main_out, prec_out):
    _, _, rows, depth = magnet.shape
    count = len(jobs)
    return pl.pallas_call(
        functools.partial(boundary_kernel, n_main, n_prec, rows, jobs),
        out_shape=[jax.ShapeDtypeStruct(main_out.shape, F32), jax.ShapeDtypeStruct(prec_out.shape, F32)],
        in_specs=[VMEM, HBM] + [VMEM] * 5 + [HBM] * 2,
        out_specs=[HBM, HBM],
        scratch_shapes=[
            pltpu.VMEM((3, count, rows, depth), F32),
            pltpu.VMEM((3, count, rows, depth), F32),
            pltpu.SemaphoreType.DMA((count,)),
            pltpu.SemaphoreType.DMA((count,)),
        ],
        input_output_aliases={7: 0, 8: 1},
        compiler_params=pltpu.CompilerParams(vmem_limit_bytes=8 << 20),
        cost_estimate=cost(len(jobs)),
        name="end_planes",
    )(flow, magnet, low, high, before, after, fed, main_out, prec_out)


def outlet_kernel(prec, plane, sem):
    copy = pltpu.make_async_copy(prec.at[:, prec.shape[1] - 1], plane, sem)
    copy.start()
    copy.wait()


def outlet(prec):
    _, _, rows, depth = prec.shape
    return pl.pallas_call(
        outlet_kernel,
        out_shape=pltpu.VMEM((3, rows, depth), F32),
        in_specs=[HBM],
        out_specs=VMEM,
        scratch_shapes=[pltpu.SemaphoreType.DMA],
        compiler_params=pltpu.CompilerParams(vmem_limit_bytes=2 << 20),
        cost_estimate=cost(1),
        name="outlet_plane",
    )(prec)


def pack_kernel(n_main, n_prec, rows, *refs):
    main, prec, row_low, row_high, low_tile, high_tile, sem = refs
    first, last = pl.ds(0, SUBLANES), pl.ds(rows - SUBLANES, SUBLANES)
    groups = [(prec, g, g) for g in range(0, n_prec, GROUP)] + [(main, g, n_prec + g) for g in range(0, n_main, GROUP)]
    copies = []
    for n, (source, x, i) in enumerate(groups):
        for m, (part, target) in enumerate(((first, low_tile), (last, high_tile))):
            copies.append(
                pltpu.make_async_copy(
                    source.at[:, pl.ds(x, GROUP), part], target.at[:, pl.ds(i, GROUP)], sem.at[2 * n + m]
                )
            )
    for copy in copies:
        copy.start()
    low_wall, high_wall, _, _ = place()
    for n, (_, _, i) in enumerate(groups):
        copies[2 * n].wait()
        copies[2 * n + 1].wait()
        for c in range(3):
            for x in range(i, i + GROUP):
                row_low[c, x] = low_tile[c, x, pl.ds(0, 1), :]
                row_high[c, x] = high_tile[c, x, pl.ds(SUBLANES - 1, 1), :]

    @pl.when(low_wall)
    def _():
        row_low[...] = jnp.zeros_like(row_low)

    @pl.when(high_wall)
    def _():
        row_high[...] = jnp.zeros_like(row_high)


def pack(main, prec):
    _, n_main, rows, depth = main.shape
    n_prec = prec.shape[1]
    total = n_main + n_prec
    packed = pltpu.VMEM((3, total, 1, depth), F32)
    return pl.pallas_call(
        functools.partial(pack_kernel, n_main, n_prec, rows),
        out_shape=[packed, packed],
        in_specs=[HBM, HBM],
        out_specs=[VMEM] * 2,
        scratch_shapes=[
            pltpu.VMEM((3, total, SUBLANES, depth), F32),
            pltpu.VMEM((3, total, SUBLANES, depth), F32),
            pltpu.SemaphoreType.DMA((2 * total // GROUP,)),
        ],
        compiler_params=pltpu.CompilerParams(vmem_limit_bytes=12 << 20),
        cost_estimate=cost(3),
        name="pack_rows",
    )(main, prec)


def relay_kernel(rows, *refs):
    order = refs[0]
    sources = refs[1:-7]
    face, theirs, held, laid, sem, out_sem = refs[-6:]
    span_index = lax.axis_index("span")
    tiles = held.shape[2]

    @pl.when(place()[3])
    def _():
        for m, source in enumerate(sources):
            for t in range(tiles):
                pltpu.make_async_copy(
                    source.at[:, :, tile_of(t)], held.at[m, :, t, pl.ds(0, rows)], sem.at[m]
                ).start()
        for c in range(3):
            for t in range(tiles):
                held[0, c, t, pl.ds(rows, SUBLANES), :] = jnp.zeros((SUBLANES, LANES), F32)
        for m in range(len(sources)):
            wait_part(held.at[m, :, :, pl.ds(0, rows)], sem.at[m])
        for k in range(2):
            base = jnp.bitwise_xor(span_index, k) * rows

            def step(r, carry, k=k, base=base):
                row = order[base + r]
                away = jnp.bitwise_xor(row // rows, span_index)
                here = away % 2 == 0
                m = jnp.where(here, away // 2, 0)
                at = jnp.where(here, row % rows, rows)
                for c in range(3):
                    for t in range(tiles):
                        laid[k, c, t, pl.ds(r, 1), :] = held[m, c, t, pl.ds(at, 1), :]
                return carry

            lax.fori_loop(0, rows, step, 0, unroll=4)
            target = face.at[:, 0] if k == 0 else theirs
            for t in range(tiles):
                pltpu.make_async_copy(laid.at[k, :, t], target.at[:, :, tile_of(t)], out_sem.at[k]).start()
        for k in range(2):
            wait_part(laid.at[k], out_sem.at[k])


def relay(order, sources, face):
    _, rows, depth = sources[0].shape
    return pl.pallas_call(
        functools.partial(relay_kernel, rows),
        out_shape=[pltpu.VMEM(face.shape, F32), pltpu.VMEM((3, rows, depth), F32)],
        in_specs=[SMEM] + [VMEM] * (len(sources) + 1),
        out_specs=[VMEM] * 2,
        scratch_shapes=[
            pltpu.VMEM((len(sources), 3, depth // LANES, rows + SUBLANES, LANES), F32),
            pltpu.VMEM((2, 3, depth // LANES, rows, LANES), F32),
            pltpu.SemaphoreType.DMA((len(sources),)),
            pltpu.SemaphoreType.DMA((2,)),
        ],
        input_output_aliases={len(sources) + 1: 0},
        compiler_params=pltpu.CompilerParams(vmem_limit_bytes=8 << 20),
        cost_estimate=cost(1),
        name="relay_rows",
    )(order, *sources, face)


def shards(main, prec, magnet, inlet_rows):
    spans = lax.axis_size("span")
    streams = lax.axis_size("stream")
    last = streams - 1
    n_main, n_prec = main.shape[1], prec.shape[1]
    main, prec, magnet = in_hbm(main), in_hbm(prec), in_hbm(magnet)
    axes = ("stream", "span")

    def hop(value, source, target, k):
        return lax.ppermute(
            value, axes, [(source * spans + a, target * spans + (a ^ k)) for a in range(spans)]
        )

    plane = outlet(prec)
    sources = [plane] + [hop(plane, last, last, 2 * m) for m in range(1, spans // 2)]
    row_low, row_high = pack(main, prec)
    up_span = [(i, (i + 1) % spans) for i in range(spans)]
    up_stream = [(i, (i + 1) % streams) for i in range(streams)]
    low = lax.ppermute(row_high, "span", up_span)
    high = lax.ppermute(row_low, "span", [(b, a) for a, b in up_span])
    *outs, flow, face_low, face_high = interior(False, main.shape, prec.shape, (main, prec, magnet))
    face_low, face_high, *sources = lax.optimization_barrier((face_low, face_high, *sources))
    face_high, theirs = relay(inlet_rows, sources, face_high)
    face_low, face_high, low, high, theirs = lax.optimization_barrier((face_low, face_high, low, high, theirs))
    fed = hop(theirs, last, 0, 1)
    before = lax.ppermute(face_high, "stream", up_stream)
    after = lax.ppermute(face_low, "stream", [(b, a) for a, b in up_stream])
    outs = interior(True, main.shape, prec.shape, (flow, magnet, low, high, *outs))
    ends = ((False, True), (False, False), (True, False), (True, True))
    outs = boundary(ends, n_main, n_prec, flow, magnet, low, high, before, after, fed, *outs)
    return tuple(outs)


def solution(mesh):
    placed = P(None, "stream", "span", None)
    return jax.shard_map(
        shards,
        mesh=mesh,
        in_specs=(placed, placed, placed, P()),
        out_specs=(placed, placed),
        check_vma=False,
    )
```

```python
import functools

import jax
import jax.numpy as jnp
from jax import lax
from jax.experimental import pallas as pl
from jax.experimental.pallas import tpu as pltpu
from jax.sharding import PartitionSpec as P

TIME_STEP = 0.1
VISCOSITY = 0.02
SMAGORINSKY = 0.03
INTERACTION = 0.5

LANES = 128
SUBLANES = 8


def cost(micros):
    return pl.CostEstimate(flops=0, bytes_accessed=int(micros * 3.7e6), transcendentals=0)


def in_hbm(value):
    return pltpu.with_memory_space_constraint(value, pltpu.HBM)


F32 = jnp.float32
ANY = pl.BlockSpec(memory_space=pl.ANY)
HBM = pl.BlockSpec(memory_space=pltpu.HBM)
VMEM = pl.BlockSpec(memory_space=pltpu.VMEM)
SMEM = pl.BlockSpec(memory_space=pltpu.SMEM)

EDDY_SCALE = (TIME_STEP * SMAGORINSKY) ** 2 / 4.0
EDDY_FLOOR = (TIME_STEP * SMAGORINSKY) ** 2 * 1e-06


def update(u, forward, backward, magnet):
    diff = [[forward[j][i] - backward[j][i] for j in range(3)] for i in range(3)]
    diag = diff[0][0] * diff[0][0] + diff[1][1] * diff[1][1] + diff[2][2] * diff[2][2]
    quad = diag + diag
    for i, j in ((0, 1), (0, 2), (1, 2)):
        pair = diff[i][j] + diff[j][i]
        quad = quad + pair * pair
    square = quad * EDDY_SCALE + EDDY_FLOOR
    eddy = square * lax.rsqrt(square)
    visc = eddy + TIME_STEP * VISCOSITY
    keep = (1.0 - 6.0 * TIME_STEP * VISCOSITY) - 6.0 * eddy
    if magnet is not None:
        scale = TIME_STEP * INTERACTION
        aligned = (u[0] * magnet[0] + u[1] * magnet[1] + u[2] * magnet[2]) * scale
        strength = magnet[0] * magnet[0] + magnet[1] * magnet[1] + magnet[2] * magnet[2]
        keep = keep - strength * scale
    speed = [u[j] * (-0.5 * TIME_STEP) for j in range(3)]
    out = []
    for i in range(3):
        around = (forward[0][i] + backward[0][i]) + (forward[1][i] + backward[1][i])
        around = around + (forward[2][i] + backward[2][i])
        value = keep * u[i] + visc * around
        value = value + speed[0] * diff[i][0] + speed[1] * diff[i][1] + speed[2] * diff[i][2]
        if magnet is not None:
            value = value + aligned * magnet[i]
        out.append(value)
    return out


def shifted_lanes(read, tiles):
    shape = (SUBLANES, LANES)
    lane = lax.broadcasted_iota(jnp.int32, shape, 1)
    zero = jnp.zeros(shape, F32)
    here = read(0)
    left = zero
    ahead = pltpu.roll(here, LANES - 1, 1)
    for t in range(tiles):
        behind = pltpu.roll(here, 1, 1)
        following = read(t + 1) if t + 1 < tiles else None
        right = pltpu.roll(following, LANES - 1, 1) if t + 1 < tiles else zero
        yield here, jnp.where(lane == LANES - 1, right, ahead), jnp.where(lane == 0, left, behind)
        here, left, ahead = following, behind, right


def plane_rows(center, low, high, before, after, magnet, store, tiles):
    streams = [shifted_lanes(lambda t, c=c: center(c, t), tiles) for c in range(3)]
    for t in range(tiles):
        along = [next(stream) for stream in streams]
        u = [value[0] for value in along]
        forward = [
            [after(c, t) for c in range(3)],
            [high(c, t) for c in range(3)],
            [value[1] for value in along],
        ]
        backward = [
            [before(c, t) for c in range(3)],
            [low(c, t) for c in range(3)],
            [value[2] for value in along],
        ]
        field = None if magnet is None else [magnet(c, t) for c in range(3)]
        for c, value in enumerate(update(u, forward, backward, field)):
            store(c, t, value)


BASE = SUBLANES
GROUP = 4


def tile_of(t):
    return pl.ds(t * LANES, LANES)


def rows_of(ref, x, at):
    return lambda c, t: ref[c, x, t, pl.ds(at, SUBLANES), :]


def span_of(ref, x, at):
    return lambda c, t: ref[c, x, pl.ds(at, SUBLANES), tile_of(t)]


def span_rows(ref, c, t, k):
    return ref[c, pl.ds(k * SUBLANES, SUBLANES), tile_of(t)]


def with_row(inside, halo, x, edge):
    def read(c, t):
        sub = lax.broadcasted_iota(jnp.int32, (SUBLANES, LANES), 0)
        row = jnp.broadcast_to(halo[c, x, :, tile_of(t)], (SUBLANES, LANES))
        return jnp.where(sub == edge, row, inside(c, t))

    return read


def edge_of(flow, low, high, x, k, last):
    at = BASE + k * SUBLANES
    below, above = rows_of(flow, x, at - 1), rows_of(flow, x, at + 1)
    if k == 0:
        below = with_row(below, low, x, 0)
    if k == last:
        above = with_row(above, high, x, SUBLANES - 1)
    return below, above


def place():
    span, stream = lax.axis_index("span"), lax.axis_index("stream")
    return span == 0, span == lax.axis_size("span") - 1, stream == 0, stream == lax.axis_size("stream") - 1


def wait_part(part, sem):
    pltpu.make_async_copy(part, part, sem).wait()


def interior_kernel(edges, n_main, n_prec, rows, *refs):
    if edges:
        flow, magnet, low, high, _, _, main_out, prec_out, field, result, field_sem, out_sem = refs
    else:
        main, prec, magnet, main_out, prec_out, flow, face_low, face_high = refs[:8]
        field, result, field_sem, out_sem, in_sem, face_sem = refs[8:]
    tiles = flow.shape[2]
    total = n_main + n_prec
    last = rows // SUBLANES - 1
    kept = [0, last] if edges else list(range(1, last))
    if edges:
        spans = [(0, 0, SUBLANES), (SUBLANES, last * SUBLANES, SUBLANES)]
    else:
        spans = [(0, SUBLANES, (last - 1) * SUBLANES)]

    def load(source, x, i):
        for t in range(tiles):
            pltpu.make_async_copy(
                source.at[:, pl.ds(x, GROUP), :, tile_of(t)],
                flow.at[:, pl.ds(i, GROUP), t, pl.ds(BASE, rows)],
                in_sem.at[i // GROUP],
            ).start()

    def load_field(x):
        for at, row, size in spans:
            pltpu.make_async_copy(
                magnet.at[:, pl.ds(x, GROUP), pl.ds(row, size)],
                field.at[:, pl.ds(x, GROUP), pl.ds(at, size)],
                field_sem.at[x // GROUP],
            ).start()

    def wait_flow(g):
        if not edges:
            wait_part(flow.at[:, pl.ds(0, GROUP), :, pl.ds(BASE, rows)], in_sem.at[g])

    def wait_field(g):
        wait_part(field.at[:, pl.ds(0, GROUP)], field_sem.at[g])

    if not edges:
        for x in range(0, n_prec, GROUP):
            load(prec, x, x)
    for x in range(0, n_main, GROUP):
        if not edges:
            load(main, x, n_prec + x)
        load_field(x)
    faces = []
    if not edges:
        for kind, source, count in ((0, main, n_main), (1, prec, n_prec)):
            faces.append((source.at[:, 0], face_low.at[:, kind]))
            faces.append((source.at[:, count - 1], face_high.at[:, kind]))
        faces = [pltpu.make_async_copy(a, b, face_sem.at[n]) for n, (a, b) in enumerate(faces)]
        for copy in faces:
            copy.start()

    def run(target, x, i, with_field):
        for n, k in enumerate(kept):
            at = BASE + k * SUBLANES

            def store(c, t, value, n=n):
                result[c, i, pl.ds(n * SUBLANES, SUBLANES), tile_of(t)] = value

            if edges:
                below, above = edge_of(flow, low, high, i, k, last)
            else:
                below, above = rows_of(flow, i, at - 1), rows_of(flow, i, at + 1)
            plane_rows(
                rows_of(flow, i, at),
                below,
                above,
                rows_of(flow, i - 1, at),
                rows_of(flow, i + 1, at),
                span_of(field, x, n * SUBLANES) if with_field else None,
                store,
                tiles,
            )
        for at, row, size in spans:
            pltpu.make_async_copy(
                result.at[:, i, pl.ds(at, size)], target.at[:, x, pl.ds(row, size)], out_sem.at[i]
            ).start()

    wait_flow(0)

    def prec_step(x, carry):
        @pl.when((x + 1) % GROUP == 0)
        def _():
            wait_flow((x + 1) // GROUP)

        run(prec_out, x, x, False)
        return carry

    lax.fori_loop(1, n_prec - 1, prec_step, 0)
    wait_flow(n_prec // GROUP)
    wait_field(0)

    def main_step(x, carry):
        @pl.when((x + 1) % GROUP == 0)
        def _():
            wait_flow((n_prec + x + 1) // GROUP)
            wait_field((x + 1) // GROUP)

        run(main_out, x, n_prec + x, True)
        return carry

    lax.fori_loop(1, n_main - 1, main_step, 0)
    for copy in faces:
        copy.wait()

    def drain(i, carry):
        wait_part(result.at[:, 0], out_sem.at[i])
        return carry

    lax.fori_loop(1, n_prec - 1, drain, 0)
    lax.fori_loop(n_prec + 1, total - 1, drain, 0)


def interior(edges, main_shape, prec_shape, operands):
    _, n_main, rows, depth = main_shape
    n_prec = prec_shape[1]
    total = n_main + n_prec
    kept = 2 * SUBLANES if edges else rows - 2 * SUBLANES
    scratch = [
        pltpu.VMEM((3, n_main, kept, depth), F32),
        pltpu.VMEM((3, total, kept, depth), F32),
        pltpu.SemaphoreType.DMA((n_main // GROUP,)),
        pltpu.SemaphoreType.DMA((total,)),
    ]
    outs = [jax.ShapeDtypeStruct(main_shape, F32), jax.ShapeDtypeStruct(prec_shape, F32)]
    out_specs = [HBM, HBM]
    if edges:
        specs = [VMEM, HBM, VMEM, VMEM, HBM, HBM]
        aliases = {4: 0, 5: 1}
    else:
        specs = [HBM] * 3
        aliases = {}
        scratch += [pltpu.SemaphoreType.DMA((total // GROUP,)), pltpu.SemaphoreType.DMA((4,))]
        outs.append(pltpu.VMEM((3, total, depth // LANES, rows + 2 * SUBLANES, LANES), F32))
        outs += [pltpu.VMEM((3, 2, rows, depth), F32)] * 2
        out_specs += [VMEM] * 3
    return pl.pallas_call(
        functools.partial(interior_kernel, edges, n_main, n_prec, rows),
        out_shape=outs,
        in_specs=specs,
        out_specs=out_specs,
        scratch_shapes=scratch,
        input_output_aliases=aliases,
        compiler_params=pltpu.CompilerParams(vmem_limit_bytes=16 << 20),
        cost_estimate=cost(8 if edges else 9),
        name="edge_rows" if edges else "inner_rows",
    )(*operands)


def boundary_kernel(n_main, n_prec, rows, jobs, parts, *refs):
    flow, magnet, low, high, before, after = refs[:6]
    inflow = refs[6 : 6 + parts]
    main_out, prec_out, field, result, field_sem, out_sem = refs[8 + parts :]
    last = rows // SUBLANES - 1
    tiles = flow.shape[2]
    at_outlet = place()[3]
    for job, (is_main, at_low) in enumerate(jobs):
        if is_main:
            x = 0 if at_low else n_main - 1
            pltpu.make_async_copy(magnet.at[:, x], field.at[:, job], field_sem.at[job]).start()
    for job, (is_main, at_low) in enumerate(jobs):
        x = 0 if at_low else (n_main if is_main else n_prec) - 1
        i = n_prec + x if is_main else x
        if is_main:
            wait_part(field.at[:, job], field_sem.at[job])
        for k in range(last + 1):
            at = BASE + k * SUBLANES
            center = rows_of(flow, i, at)
            face = span_of(before if at_low else after, 0 if is_main else 1, k * SUBLANES)

            def store(c, t, value, job=job, k=k):
                result[c, job, pl.ds(k * SUBLANES, SUBLANES), tile_of(t)] = value

            def inlet(c, t, k=k, face=face):
                return face(c, t) + span_rows(inflow[0], c, t, k)

            def outlet(c, t, center=center, face=face):
                return jnp.where(at_outlet, center(c, t), face(c, t))

            if is_main:
                face_side = inlet if at_low else outlet
            else:
                face_side = face
            below, above = edge_of(flow, low, high, i, k, last)
            plane_rows(
                center,
                below,
                above,
                face_side if at_low else rows_of(flow, i - 1, at),
                rows_of(flow, i + 1, at) if at_low else face_side,
                span_of(field, job, k * SUBLANES) if is_main else None,
                store,
                tiles,
            )
        target = main_out if is_main else prec_out
        pltpu.make_async_copy(result.at[:, job], target.at[:, x], out_sem.at[job]).start()
    for job in range(len(jobs)):
        wait_part(result.at[:, job], out_sem.at[job])


def boundary(jobs, n_main, n_prec, flow, magnet, low, high, before, after, inflow, main_out, prec_out):
    _, _, rows, depth = magnet.shape
    count = len(jobs)
    return pl.pallas_call(
        functools.partial(boundary_kernel, n_main, n_prec, rows, jobs, len(inflow)),
        out_shape=[jax.ShapeDtypeStruct(main_out.shape, F32), jax.ShapeDtypeStruct(prec_out.shape, F32)],
        in_specs=[VMEM, HBM] + [VMEM] * (4 + len(inflow)) + [HBM] * 2,
        out_specs=[HBM, HBM],
        scratch_shapes=[
            pltpu.VMEM((3, count, rows, depth), F32),
            pltpu.VMEM((3, count, rows, depth), F32),
            pltpu.SemaphoreType.DMA((count,)),
            pltpu.SemaphoreType.DMA((count,)),
        ],
        input_output_aliases={6 + len(inflow): 0, 7 + len(inflow): 1},
        compiler_params=pltpu.CompilerParams(vmem_limit_bytes=8 << 20),
        cost_estimate=cost(len(jobs)),
        name="end_planes" if count > 1 else "inlet_plane",
    )(flow, magnet, low, high, before, after, *inflow, main_out, prec_out)


def outlet_kernel(prec, plane, sem):
    copy = pltpu.make_async_copy(prec.at[:, prec.shape[1] - 1], plane, sem)
    copy.start()
    copy.wait()


def outlet(prec):
    _, _, rows, depth = prec.shape
    return pl.pallas_call(
        outlet_kernel,
        out_shape=pltpu.VMEM((3, rows, depth), F32),
        in_specs=[HBM],
        out_specs=VMEM,
        scratch_shapes=[pltpu.SemaphoreType.DMA],
        compiler_params=pltpu.CompilerParams(vmem_limit_bytes=2 << 20),
        cost_estimate=cost(1),
        name="outlet_plane",
    )(prec)


def pack_kernel(n_main, n_prec, rows, *refs):
    main, prec, row_low, row_high, low_tile, high_tile, sem = refs
    first, last = pl.ds(0, SUBLANES), pl.ds(rows - SUBLANES, SUBLANES)
    groups = [(prec, g, g) for g in range(0, n_prec, GROUP)] + [(main, g, n_prec + g) for g in range(0, n_main, GROUP)]
    copies = []
    for n, (source, x, i) in enumerate(groups):
        for m, (part, target) in enumerate(((first, low_tile), (last, high_tile))):
            copies.append(
                pltpu.make_async_copy(
                    source.at[:, pl.ds(x, GROUP), part], target.at[:, pl.ds(i, GROUP)], sem.at[2 * n + m]
                )
            )
    for copy in copies:
        copy.start()
    low_wall, high_wall, _, _ = place()
    for n, (_, _, i) in enumerate(groups):
        copies[2 * n].wait()
        copies[2 * n + 1].wait()
        for c in range(3):
            for x in range(i, i + GROUP):
                row_low[c, x] = low_tile[c, x, pl.ds(0, 1), :]
                row_high[c, x] = high_tile[c, x, pl.ds(SUBLANES - 1, 1), :]

    @pl.when(low_wall)
    def _():
        row_low[...] = jnp.zeros_like(row_low)

    @pl.when(high_wall)
    def _():
        row_high[...] = jnp.zeros_like(row_high)


def pack(main, prec):
    _, n_main, rows, depth = main.shape
    n_prec = prec.shape[1]
    total = n_main + n_prec
    packed = pltpu.VMEM((3, total, 1, depth), F32)
    return pl.pallas_call(
        functools.partial(pack_kernel, n_main, n_prec, rows),
        out_shape=[packed, packed],
        in_specs=[HBM, HBM],
        out_specs=[VMEM] * 2,
        scratch_shapes=[
            pltpu.VMEM((3, total, SUBLANES, depth), F32),
            pltpu.VMEM((3, total, SUBLANES, depth), F32),
            pltpu.SemaphoreType.DMA((2 * total // GROUP,)),
        ],
        compiler_params=pltpu.CompilerParams(vmem_limit_bytes=12 << 20),
        cost_estimate=cost(3),
        name="pack_rows",
    )(main, prec)


def relay_kernel(rows, *refs):
    order = refs[0]
    sources = refs[1:-7]
    face, theirs, held, laid, sem, out_sem = refs[-6:]
    span_index = lax.axis_index("span")
    tiles = held.shape[2]

    @pl.when(place()[3])
    def _():
        for m, source in enumerate(sources):
            for t in range(tiles):
                pltpu.make_async_copy(
                    source.at[:, :, tile_of(t)], held.at[m, :, t, pl.ds(0, rows)], sem.at[m]
                ).start()
        for c in range(3):
            for t in range(tiles):
                held[0, c, t, pl.ds(rows, SUBLANES), :] = jnp.zeros((SUBLANES, LANES), F32)
        for m in range(len(sources)):
            wait_part(held.at[m, :, :, pl.ds(0, rows)], sem.at[m])
        for k in range(2):
            base = jnp.bitwise_xor(span_index, k) * rows

            def step(r, carry, k=k, base=base):
                row = order[base + r]
                away = jnp.bitwise_xor(row // rows, span_index)
                here = away % 2 == 0
                m = jnp.where(here, away // 2, 0)
                at = jnp.where(here, row % rows, rows)
                for c in range(3):
                    for t in range(tiles):
                        laid[k, c, t, pl.ds(r, 1), :] = held[m, c, t, pl.ds(at, 1), :]
                return carry

            lax.fori_loop(0, rows, step, 0, unroll=4)
            target = face.at[:, 0] if k == 0 else theirs
            for t in range(tiles):
                pltpu.make_async_copy(laid.at[k, :, t], target.at[:, :, tile_of(t)], out_sem.at[k]).start()
        for k in range(2):
            wait_part(laid.at[k], out_sem.at[k])


def relay(order, sources, face):
    _, rows, depth = sources[0].shape
    return pl.pallas_call(
        functools.partial(relay_kernel, rows),
        out_shape=[pltpu.VMEM(face.shape, F32), pltpu.VMEM((3, rows, depth), F32)],
        in_specs=[SMEM] + [VMEM] * (len(sources) + 1),
        out_specs=[VMEM] * 2,
        scratch_shapes=[
            pltpu.VMEM((len(sources), 3, depth // LANES, rows + SUBLANES, LANES), F32),
            pltpu.VMEM((2, 3, depth // LANES, rows, LANES), F32),
            pltpu.SemaphoreType.DMA((len(sources),)),
            pltpu.SemaphoreType.DMA((2,)),
        ],
        input_output_aliases={len(sources) + 1: 0},
        compiler_params=pltpu.CompilerParams(vmem_limit_bytes=8 << 20),
        cost_estimate=cost(1),
        name="relay_rows",
    )(order, *sources, face)


def shards(main, prec, magnet, inlet_rows):
    spans = lax.axis_size("span")
    streams = lax.axis_size("stream")
    last = streams - 1
    n_main, n_prec = main.shape[1], prec.shape[1]
    main, prec, magnet = in_hbm(main), in_hbm(prec), in_hbm(magnet)
    axes = ("stream", "span")

    def hop(value, source, target, k):
        return lax.ppermute(
            value, axes, [(source * spans + a, target * spans + (a ^ k)) for a in range(spans)]
        )

    plane = outlet(prec)
    sources = [plane] + [hop(plane, last, last, 2 * m) for m in range(1, spans // 2)]
    row_low, row_high = pack(main, prec)
    up_span = [(i, (i + 1) % spans) for i in range(spans)]
    up_stream = [(i, (i + 1) % streams) for i in range(streams)]
    low = lax.ppermute(row_high, "span", up_span)
    high = lax.ppermute(row_low, "span", [(b, a) for a, b in up_span])
    *outs, flow, face_low, face_high = interior(False, main.shape, prec.shape, (main, prec, magnet))
    face_low, face_high, *sources = lax.optimization_barrier((face_low, face_high, *sources))
    face_high, theirs = relay(inlet_rows, sources, face_high)
    face_low, face_high, low, high, theirs = lax.optimization_barrier((face_low, face_high, low, high, theirs))
    fed = hop(theirs, last, 0, 1)
    before = lax.ppermute(face_high, "stream", up_stream)
    after = lax.ppermute(face_low, "stream", [(b, a) for a, b in up_stream])
    outs = interior(True, main.shape, prec.shape, (flow, magnet, low, high, *outs))
    ends = ((False, True), (False, False), (True, False))
    outs = boundary(ends, n_main, n_prec, flow, magnet, low, high, before, after, (), *outs)
    outs = boundary(((True, True),), n_main, n_prec, flow, magnet, low, high, before, after, (fed,), *outs)
    return tuple(outs)


def solution(mesh):
    placed = P(None, "stream", "span", None)
    return jax.shard_map(
        shards,
        mesh=mesh,
        in_specs=(placed, placed, placed, P()),
        out_specs=(placed, placed),
        check_vma=False,
    )
```
